32 devices in a mesh: grp: 2 (over x), leaf: 8 (over z, y), sub: 2 (over core).
Axes of the slice: x: 2, y: 2, z: 4, core: 2. Of those that a mesh axis runs over, the one named last changes fastest.
Arguments:
- right_side: float32 [512, 2048], P(('grp', 'leaf', 'sub')), parts along dimension 0, may hold values from -24 to 24, as said below
- first_guess: float32 [512, 2048], P(('grp', 'leaf', 'sub')), parts along dimension 0, may hold values from -3 to 3
- couple: bfloat16 [512, 64, 384], P(('grp', 'leaf', 'sub')), parts along dimension 0, may hold values from -0.75 to 0.75
- send_lists: int32 [32, 2, 4], P(('grp', 'leaf', 'sub')), parts along dimension 0, may hold values from -1 to 15, as said below
- neighbours: int32 [512, 6], P(('grp', 'leaf', 'sub')), parts along dimension 0, may hold values from -1 to 23, as said below
Outputs:
- solution: float32 [512, 2048], P(('grp', 'leaf', 'sub')), parts along dimension 0
- residual: float32 [512, 2048], P(('grp', 'leaf', 'sub')), parts along dimension 0
The draws below stay inside these ranges and needn't reach their ends.
There are 2 independent parts, one for each index of `grp`. The reference program is written for one: setup_inputs(seed, part) draws one part's arguments, and reference() takes and returns one part's arrays. A program takes and returns all parts, laid end to end along the dimension named above; each array names one. Nothing has to cross between parts.
Inputs may be any that keep to these rules, and one draw needn't show every extreme that they name: `right_side`: rows rise in scale along the element order. `send_lists`: for device d of a part and direction 0 (toward device d + 1) or 1 (toward device d - 1): distinct local element indices in the live slots, which come first, and -1 after them. The first device sends nothing in direction 1, the last nothing in direction 0; some device fills all 4 slots in direction 0 and the device after it all 4 in direction 1. `neighbours`: positions below 16 are the device's own elements, 16 + s the live slot s received from the previous device, 20 + s the live slot s received from the next device; -1 marks a face on the band's boundary.
All inputs are finite; a program needn't handle non-finite values.
Results may differ from the reference program's by a relative error of at most 0.034.
Values may be sent and summed in bfloat16 or wider, within the bound.
A program may use at most 64 MiB of HBM per device.

```python
import math
import jax
import jax.numpy as jnp
from jax import lax

DOF = 64
FACES = 6
RHS = 32
SSTEP = 3
CYCLES = 4
E_DEV = 16
SLOTS = 4
DEVS_PART = 16
ELEMS = 256


def send_counts(key):
    device_count = DEVS_PART
    counts = jax.random.randint(jax.random.fold_in(key, 7), (device_count, 2), SLOTS // 4, SLOTS + 1)
    chosen = jax.random.randint(jax.random.fold_in(key, 8), (), 0, device_count - 1)
    places = jnp.arange(device_count)
    counts = counts.at[:, 0].set(jnp.where(places == chosen, SLOTS, counts[:, 0]))
    counts = counts.at[:, 1].set(jnp.where(places == chosen + 1, SLOTS, counts[:, 1]))
    counts = counts.at[device_count - 1, 0].set(0)
    counts = counts.at[0, 1].set(0)
    return (counts.astype(jnp.int32), chosen.astype(jnp.int32))


def draw_send_lists(key, part):
    counts, chosen = send_counts(key)
    keys = jax.random.split(jax.random.fold_in(key, 11), DEVS_PART * 2)

    def offsets(one_key):
        mixed = jax.random.permutation(one_key, 2 * SLOTS - 1)[:SLOTS - 1] + 1
        return jnp.concatenate([jnp.zeros((1,), jnp.int32), mixed.astype(jnp.int32)])
    table = jax.vmap(offsets)(keys).reshape(DEVS_PART, 2, SLOTS)
    local = jnp.stack([E_DEV - 1 - table[:, 0], table[:, 1]], axis=1)
    slot_ids = jnp.arange(SLOTS)[None, None, :]
    return jnp.where(slot_ids < counts[:, :, None], local, -1).astype(jnp.int32)


def draw_neighbours(key, part):
    counts, chosen = send_counts(key)
    shape = (ELEMS, FACES)
    kinds = jax.random.randint(jax.random.fold_in(key, 21), shape, 0, 100)
    local = jax.random.randint(jax.random.fold_in(key, 22), shape, 0, E_DEV)
    drawn = jax.random.randint(jax.random.fold_in(key, 23), shape, 0, 1 << 20)
    device = (jnp.arange(ELEMS) // E_DEV)[:, None]
    before_count = jnp.where(device > 0, counts[jnp.maximum(device - 1, 0), 0], 0)
    after_count = jnp.where(device < DEVS_PART - 1, counts[jnp.minimum(device + 1, DEVS_PART - 1), 1], 0)
    before = jnp.where(before_count > 0, E_DEV + drawn % jnp.maximum(before_count, 1), -1)
    after = jnp.where(after_count > 0, E_DEV + SLOTS + drawn % jnp.maximum(after_count, 1), -1)
    result = jnp.where(kinds < 8, -1, jnp.where(kinds < 76, local, jnp.where(kinds < 88, before, after)))
    result = result.at[chosen * E_DEV, 0].set(E_DEV + 2 * SLOTS - 1)
    result = result.at[(chosen + 1) * E_DEV, 1].set(E_DEV + SLOTS - 1)
    return result.astype(jnp.int32)


def draw_couple(key, part):
    shape = (ELEMS, DOF, FACES * DOF)
    scale = 0.85 / math.sqrt(FACES * DOF)
    strength = jnp.exp(jax.random.uniform(jax.random.fold_in(key, 31), (ELEMS, 1, 1), jnp.float32, math.log(0.5), math.log(1.5)))
    values = jnp.clip(jax.random.normal(jax.random.fold_in(key, 32), shape, jnp.float32), -4.0, 4.0)
    return (values * scale * strength).astype(jnp.bfloat16)


def draw_right_side(key, part):
    ramp = 0.5 + jnp.arange(ELEMS, dtype=jnp.float32) / max(ELEMS - 1, 1)
    shape = (ELEMS, DOF, RHS)
    values = jnp.clip(jax.random.normal(jax.random.fold_in(key, 41), shape, jnp.float32), -4.0, 4.0)
    return (values * ramp[:, None, None]).reshape(ELEMS, DOF * RHS).astype(jnp.float32)


def steps_of(stream_key, dims, cuts, least, top_value):
    factor_of = 1.0
    for axis_at, shards_of in cuts:
        steps = jax.random.uniform(jax.random.fold_in(jax.random.fold_in(stream_key, 6), axis_at), (shards_of,), jnp.float32, least / len(cuts), top_value / len(cuts))
        factor_of = factor_of * jnp.repeat(jnp.exp(steps), dims[axis_at] // shards_of).reshape((-1,) + (1,) * (len(dims) - 1 - axis_at))
    return factor_of


def normal_values(key, shape, spread, most, pieces=(), kind=jnp.bfloat16):
    values = spread * jax.random.normal(key, shape, jnp.float32)
    if pieces:
        values = values * steps_of(key, shape, pieces, -0.22, 0.18)
    return jnp.clip(values, -most, most).astype(kind)


def setup_inputs(seed: int = 0, part: int = 0) -> dict:
    streams_of = jax.random.split(jax.random.key(seed), 6)
    part_keys = jax.random.split(jax.random.fold_in(streams_of[5], part), 6)
    return {
        "right_side": draw_right_side(jax.random.fold_in(jax.random.fold_in(streams_of[5], part), 71), part),
        "first_guess": normal_values(part_keys[1], (ELEMS, DOF * RHS), 0.5, 3.0, ((0, 16),), jnp.float32),
        "couple": draw_couple(jax.random.fold_in(jax.random.fold_in(streams_of[5], part), 71), part),
        "send_lists": draw_send_lists(jax.random.fold_in(jax.random.fold_in(streams_of[5], part), 71), part),
        "neighbours": draw_neighbours(jax.random.fold_in(jax.random.fold_in(streams_of[5], part), 71), part),
    }


def couple_apply(vector_field, couple, send_lists, neighbours):
    device_count = send_lists.shape[0]
    row_width = vector_field.shape[1]
    blocks = vector_field.astype(jnp.bfloat16).reshape(device_count, E_DEV, row_width)

    def listed_blocks(direction):
        listed = send_lists[:, direction, :]
        chosen = jnp.take_along_axis(blocks, jnp.maximum(listed, 0).astype(jnp.int32)[:, :, None], axis=1)
        return jnp.where(listed[:, :, None] >= 0, chosen, jnp.zeros_like(chosen))
    forward = listed_blocks(0)
    backward = listed_blocks(1)
    empty_row = jnp.zeros((1, SLOTS, row_width), jnp.bfloat16)
    before_blocks = jnp.concatenate([empty_row, forward[:-1]], axis=0)
    after_blocks = jnp.concatenate([backward[1:], empty_row], axis=0)
    zero_block = jnp.zeros((device_count, 1, row_width), jnp.bfloat16)
    extended = jnp.concatenate([blocks, before_blocks, after_blocks, zero_block], axis=1)
    positions = neighbours.reshape(device_count, E_DEV * FACES)
    positions = jnp.where(positions < 0, E_DEV + 2 * SLOTS, positions).astype(jnp.int32)
    coupling = couple.reshape(device_count, E_DEV, DOF, FACES * DOF)

    def one_device(operands):
        own_extended, own_positions, own_coupling = operands
        gathered = jnp.take(own_extended, own_positions, axis=0).reshape(E_DEV, FACES * DOF, RHS)
        product = jnp.einsum('eik,ekr->eir', own_coupling.astype(jnp.float32), gathered.astype(jnp.float32))
        return product.reshape(E_DEV, DOF * RHS)
    result = lax.map(one_device, (extended, positions, coupling))
    return result.reshape(device_count * E_DEV, DOF * RHS)

def to_columns(vector_field):
    return vector_field.reshape(-1, RHS)

def reference(right_side, first_guess, couple, send_lists, neighbours):
    solution = first_guess
    residual = right_side - first_guess + couple_apply(first_guess, couple, send_lists, neighbours)
    for repeat in range(CYCLES):
        krylov_blocks = [residual]
        for degree in range(SSTEP):
            krylov_blocks.append(couple_apply(krylov_blocks[-1], couple, send_lists, neighbours))
        images = [krylov_blocks[order_index] - krylov_blocks[order_index + 1] for order_index in range(SSTEP)]
        stacked = jnp.concatenate([to_columns(image_block) for image_block in images] + [to_columns(residual)], axis=1)
        gram_matrix = jnp.dot(stacked.T.astype(jnp.float32), stacked.astype(jnp.float32), precision=lax.Precision.HIGHEST, preferred_element_type=jnp.float32)
        square_block = gram_matrix[:SSTEP * RHS, :SSTEP * RHS]
        right_block = gram_matrix[:SSTEP * RHS, SSTEP * RHS:]
        factor = jnp.linalg.cholesky(square_block)
        coeffs = jax.scipy.linalg.cho_solve((factor, True), right_block)
        krylov = jnp.concatenate([to_columns(basis_block) for basis_block in krylov_blocks[:SSTEP]], axis=1)
        solution = solution + jnp.dot(krylov.astype(jnp.float32), coeffs.astype(jnp.float32), precision=lax.Precision.HIGHEST, preferred_element_type=jnp.float32).reshape(solution.shape)
        residual = residual - jnp.dot(stacked[:, :SSTEP * RHS].astype(jnp.float32), coeffs.astype(jnp.float32), precision=lax.Precision.HIGHEST, preferred_element_type=jnp.float32).reshape(residual.shape)
    return (solution, residual)
```

```python
import functools

import jax
import jax.numpy as jnp
from jax import lax
from jax.experimental import pallas as pl
from jax.experimental.pallas import tpu as pltpu
from jax.sharding import PartitionSpec as P

DOF = 64
FACES = 6
RHS = 32
SSTEP = 3
CYCLES = 4
KEPT = SSTEP * RHS
WIDTH = KEPT + RHS
MESH = pl.DeviceIdType.MESH


def gauss_jordan(system):
    rows = lax.broadcasted_iota(jnp.int32, (KEPT, 1), 0)
    for k in range(KEPT):
        pivot_row = system[k : k + 1, :] / system[k : k + 1, k : k + 1]
        system = jnp.where(rows == k, pivot_row, system - system[:, k : k + 1] * pivot_row)
    return system[:, KEPT:]


def split(value):
    high = value.astype(jnp.bfloat16)
    return high, (value - high.astype(jnp.float32)).astype(jnp.bfloat16)


def kernel(
    leaves, subs, elems, slots,
    right_ref, guess_ref, couple_ref, lists_ref, near_ref,
    x_ref, r_ref,
    ext, basis, current, packed_out, packed_in, partial, arrived, total,
    halo_send, halo_recv, sum_send, sum_recv,
):
    count = leaves * subs
    share = WIDTH // count
    zero_at = elems + 2 * slots
    me = lax.axis_index("leaf") * subs + lax.axis_index("sub")

    def place(index):
        return {"leaf": lax.div(index, subs), "sub": lax.rem(index, subs)}

    def peer(step):
        return lax.rem(me + step, count)

    barrier = pltpu.get_barrier_semaphore()
    for step in range(1, count):
        pl.semaphore_signal(barrier, inc=1, device_id=place(peer(step)), device_id_type=MESH)
    pl.semaphore_wait(barrier, count - 1)

    for side in range(2):
        ext[side, elems:] = jnp.zeros((2 * slots + 1, DOF, RHS), jnp.bfloat16)

    def halo_copy(way, at, target):
        return pltpu.make_async_remote_copy(
            src_ref=packed_out.at[at, way],
            dst_ref=packed_in.at[at, way],
            send_sem=halo_send.at[at, way],
            recv_sem=halo_recv.at[at, way],
            device_id=place(target),
            device_id_type=MESH,
        )

    def exchange(side, at):
        for way in range(2):
            blocks = []
            for slot in range(slots):
                listed = lists_ref[0, way, slot]
                blocks.append(ext[side, jnp.where(listed < 0, zero_at, listed)])
            packed_out[at, way] = jnp.concatenate(blocks, axis=1)
        ahead = halo_copy(0, at, lax.rem(me + 1, count))
        back = halo_copy(1, at, lax.rem(me + count - 1, count))
        has_next = me < count - 1
        has_previous = me > 0

        @pl.when(has_next)
        def _():
            ahead.start()

        @pl.when(has_previous)
        def _():
            back.start()

        @pl.when(has_previous)
        def _():
            ahead.wait_recv()
            for slot in range(slots):
                ext[side, elems + slot] = packed_in[at, 0, :, slot * RHS : (slot + 1) * RHS]

        @pl.when(has_next)
        def _():
            back.wait_recv()
            for slot in range(slots):
                ext[side, elems + slots + slot] = packed_in[at, 1, :, slot * RHS : (slot + 1) * RHS]

        @pl.when(has_next)
        def _():
            ahead.wait_send()

        @pl.when(has_previous)
        def _():
            back.wait_send()

    def applied(side, element):
        blocks = []
        for face in range(FACES):
            near = near_ref[element, face]
            blocks.append(ext[side, jnp.where(near < 0, zero_at, near)])
        gathered = jnp.concatenate(blocks, axis=0)
        return jnp.dot(couple_ref[element], gathered, preferred_element_type=jnp.float32)

    def rows_of(element):
        return slice(element * DOF, (element + 1) * DOF)

    def keep(rows, order, value):
        high, low = split(value)
        basis[rows, order * RHS : (order + 1) * RHS] = high
        basis[rows, WIDTH + order * RHS : WIDTH + (order + 1) * RHS] = low
        return high

    for element in range(elems):
        guess = guess_ref[rows_of(element), :]
        x_ref[rows_of(element), :] = guess
        ext[1, element] = guess.astype(jnp.bfloat16)
    exchange(1, SSTEP)
    for element in range(elems):
        rows = rows_of(element)
        first = right_ref[rows, :] - guess_ref[rows, :] + applied(1, element)
        r_ref[rows, :] = first
        ext[0, element] = keep(rows, SSTEP, first)

    def sum_copy(source, target, step, phase):
        return pltpu.make_async_remote_copy(
            src_ref=source,
            dst_ref=target,
            send_sem=sum_send.at[phase],
            recv_sem=sum_recv.at[phase],
            device_id=place(peer(step)),
            device_id_type=MESH,
        )

    def cycle(repeat, carry):
        for order in range(SSTEP):
            side = order % 2
            exchange(side, order)
            for element in range(elems):
                rows = rows_of(element)
                image = applied(side, element)
                before = r_ref[rows, :] if order == 0 else current[rows, :]
                keep(rows, order, before - image)
                if order < SSTEP - 1:
                    current[rows, :] = image
                    ext[1 - side, element] = image.astype(jnp.bfloat16)

        products = lax.dot_general(
            basis[:, :WIDTH], basis[...], (((0,), (0,)), ((), ())),
            preferred_element_type=jnp.float32,
        )
        cross = products[:, WIDTH:]
        gram = products[:, :WIDTH] + cross + cross.T
        for shard in range(count):
            partial[shard] = gram[shard * share : (shard + 1) * share, :]
        for step in range(1, count):
            sum_copy(partial.at[peer(step)], arrived.at[step], step, 0).start()
        rest = pl.ds(1, count - 1)
        whole = sum_copy(partial.at[rest], arrived.at[rest], 1, 0)
        whole.wait_recv()
        reduced = partial[me]
        for step in range(1, count):
            reduced = reduced + arrived[step]
        total[me] = reduced
        for step in range(1, count):
            sum_copy(total.at[me], total.at[me], step, 1).start()
        whole.wait_send()
        both = sum_copy(total.at[rest], total.at[rest], 1, 1)
        both.wait_recv()
        both.wait_send()
        system = jnp.concatenate(
            [total[shard] for shard in range(count)], axis=0
        )[:KEPT]
        coeffs = gauss_jordan(system)

        c0, c1, c2 = coeffs[:RHS], coeffs[RHS : 2 * RHS], coeffs[2 * RHS :]
        nothing = jnp.zeros((RHS, RHS), jnp.float32)
        late = c1 + c2
        down = jnp.concatenate([c0, c1, c2, nothing], axis=0)
        up = jnp.concatenate([-late, -c2, nothing, c0 + late], axis=0)
        high, low = split(jnp.concatenate([down, up], axis=1))
        factor = jnp.concatenate(
            [
                jnp.concatenate([high, low], axis=1),
                jnp.concatenate([high, jnp.zeros_like(low)], axis=1),
            ],
            axis=0,
        )
        for element in range(elems):
            rows = rows_of(element)
            change = jnp.dot(basis[rows, :], factor, preferred_element_type=jnp.float32)
            change = change[:, : 2 * RHS] + change[:, 2 * RHS :]
            x_ref[rows, :] = x_ref[rows, :] + change[:, RHS:]
            later = r_ref[rows, :] - change[:, :RHS]
            r_ref[rows, :] = later
            ext[0, element] = keep(rows, SSTEP, later)
        return carry

    lax.fori_loop(0, CYCLES, cycle, 0)


def shards(leaves, subs, right_side, first_guess, couple, send_lists, neighbours):
    elems, _, _ = couple.shape
    slots = send_lists.shape[2]
    count = leaves * subs
    share = WIDTH // count
    rows = elems * DOF
    vmem = pl.BlockSpec(memory_space=pltpu.VMEM)
    smem = pl.BlockSpec(memory_space=pltpu.SMEM)
    field = jax.ShapeDtypeStruct((rows, RHS), jnp.float32)
    x, r = pl.pallas_call(
        functools.partial(kernel, leaves, subs, elems, slots),
        out_shape=(field, field),
        in_specs=[vmem, vmem, vmem, smem, smem],
        out_specs=(vmem, vmem),
        scratch_shapes=[
            pltpu.VMEM((2, elems + 2 * slots + 1, DOF, RHS), jnp.bfloat16),
            pltpu.VMEM((rows, 2 * WIDTH), jnp.bfloat16),
            pltpu.VMEM((rows, RHS), jnp.float32),
            pltpu.VMEM((SSTEP + 1, 2, DOF, slots * RHS), jnp.bfloat16),
            pltpu.VMEM((SSTEP + 1, 2, DOF, slots * RHS), jnp.bfloat16),
            pltpu.VMEM((count, share, WIDTH), jnp.float32),
            pltpu.VMEM((count, share, WIDTH), jnp.float32),
            pltpu.VMEM((count, share, WIDTH), jnp.float32),
            pltpu.SemaphoreType.DMA((SSTEP + 1, 2)),
            pltpu.SemaphoreType.DMA((SSTEP + 1, 2)),
            pltpu.SemaphoreType.DMA((2,)),
            pltpu.SemaphoreType.DMA((2,)),
        ],
        compiler_params=pltpu.CompilerParams(
            collective_id=0, has_side_effects=True, vmem_limit_bytes=40 * 1024 * 1024
        ),
    )(
        right_side.reshape(rows, RHS), first_guess.reshape(rows, RHS),
        couple, send_lists, neighbours,
    )
    return x.reshape(right_side.shape), r.reshape(right_side.shape)


def solution(mesh):
    lead = ("grp", "leaf", "sub")
    flat, deep = P(lead, None), P(lead, None, None)
    return jax.shard_map(
        functools.partial(shards, mesh.shape["leaf"], mesh.shape["sub"]),
        mesh=mesh,
        in_specs=(flat, flat, deep, deep, flat),
        out_specs=(flat, flat),
        check_vma=False,
    )
```

```python
import functools

import jax
import jax.numpy as jnp
from jax import lax
from jax.experimental import pallas as pl
from jax.experimental.pallas import tpu as pltpu
from jax.sharding import PartitionSpec as P

DOF = 64
FACES = 6
RHS = 32
SSTEP = 3
CYCLES = 4
KEPT = SSTEP * RHS
WIDTH = KEPT + RHS
MESH = pl.DeviceIdType.MESH


def gauss_jordan(system):
    tile = 8
    tiles = [system[first : first + tile] for first in range(0, KEPT, tile)]
    rows = lax.broadcasted_iota(jnp.int32, (tile, WIDTH), 0)

    def columns(value, at):
        first = at * tile
        return [
            jnp.broadcast_to(value[:, first + k : first + k + 1], (tile, WIDTH))
            for k in range(tile)
        ]

    for at in range(len(tiles)):
        block, factors = tiles[at], columns(tiles[at], at)
        outside = [columns(value, at) if i != at else None for i, value in enumerate(tiles)]
        for k in range(tile):
            inverse = 1.0 / factors[k][k : k + 1, :]

            def eliminated(value):
                pivot_row = value[k : k + 1, :] * inverse
                return jnp.where(rows == k, pivot_row, value - factors[k] * pivot_row)

            block = eliminated(block)
            factors = factors[: k + 1] + [eliminated(value) for value in factors[k + 1 :]]
        tiles[at] = block
        for i in range(len(tiles)):
            if i != at:
                value = tiles[i]
                for k in range(tile):
                    value = value - outside[i][k] * block[k : k + 1, :]
                tiles[i] = value
    return jnp.concatenate(tiles, axis=0)[:, KEPT:]


def split(value):
    high = value.astype(jnp.bfloat16)
    return high, (value - high.astype(jnp.float32)).astype(jnp.bfloat16)


def kernel(
    leaves, subs, elems, slots,
    right_ref, guess_ref, couple_ref, lists_ref, near_ref,
    x_ref, r_ref,
    ext, basis, current, packed_out, packed_in, partial, arrived, total,
    halo_send, halo_recv, sum_send, sum_recv,
):
    count = leaves * subs
    share = WIDTH // count
    zero_at = elems + 2 * slots
    me = lax.axis_index("leaf") * subs + lax.axis_index("sub")

    def place(index):
        return {"leaf": lax.div(index, subs), "sub": lax.rem(index, subs)}

    def peer(step):
        return lax.rem(me + step, count)

    barrier = pltpu.get_barrier_semaphore()
    for step in range(1, count):
        pl.semaphore_signal(barrier, inc=1, device_id=place(peer(step)), device_id_type=MESH)
    pl.semaphore_wait(barrier, count - 1)

    for side in range(2):
        ext[side, elems:] = jnp.zeros((2 * slots + 1, DOF, RHS), jnp.bfloat16)

    def halo_copy(way, at, target):
        return pltpu.make_async_remote_copy(
            src_ref=packed_out.at[at, way],
            dst_ref=packed_in.at[at, way],
            send_sem=halo_send.at[at, way],
            recv_sem=halo_recv.at[at, way],
            device_id=place(target),
            device_id_type=MESH,
        )

    def exchange(side, at):
        for way in range(2):
            blocks = []
            for slot in range(slots):
                listed = lists_ref[0, way, slot]
                blocks.append(ext[side, jnp.where(listed < 0, zero_at, listed)])
            packed_out[at, way] = jnp.concatenate(blocks, axis=1)
        ahead = halo_copy(0, at, lax.rem(me + 1, count))
        back = halo_copy(1, at, lax.rem(me + count - 1, count))
        has_next = me < count - 1
        has_previous = me > 0

        @pl.when(has_next)
        def _():
            ahead.start()

        @pl.when(has_previous)
        def _():
            back.start()

        @pl.when(has_previous)
        def _():
            ahead.wait_recv()
            for slot in range(slots):
                ext[side, elems + slot] = packed_in[at, 0, :, slot * RHS : (slot + 1) * RHS]

        @pl.when(has_next)
        def _():
            back.wait_recv()
            for slot in range(slots):
                ext[side, elems + slots + slot] = packed_in[at, 1, :, slot * RHS : (slot + 1) * RHS]

        @pl.when(has_next)
        def _():
            ahead.wait_send()

        @pl.when(has_previous)
        def _():
            back.wait_send()

    def applied(side, element):
        blocks = []
        for face in range(FACES):
            near = near_ref[element, face]
            blocks.append(ext[side, jnp.where(near < 0, zero_at, near)])
        gathered = jnp.concatenate(blocks, axis=0)
        return jnp.dot(couple_ref[element], gathered, preferred_element_type=jnp.float32)

    def rows_of(element):
        return slice(element * DOF, (element + 1) * DOF)

    def keep(rows, order, value):
        high, low = split(value)
        basis[rows, order * RHS : (order + 1) * RHS] = high
        basis[rows, WIDTH + order * RHS : WIDTH + (order + 1) * RHS] = low
        return high

    for element in range(elems):
        guess = guess_ref[rows_of(element), :]
        x_ref[rows_of(element), :] = guess
        ext[1, element] = guess.astype(jnp.bfloat16)
    exchange(1, SSTEP)
    for element in range(elems):
        rows = rows_of(element)
        first = right_ref[rows, :] - guess_ref[rows, :] + applied(1, element)
        r_ref[rows, :] = first
        ext[0, element] = keep(rows, SSTEP, first)

    def sum_copy(source, target, step, phase):
        return pltpu.make_async_remote_copy(
            src_ref=source,
            dst_ref=target,
            send_sem=sum_send.at[phase],
            recv_sem=sum_recv.at[phase],
            device_id=place(peer(step)),
            device_id_type=MESH,
        )

    def cycle(repeat, carry):
        for order in range(SSTEP):
            side = order % 2
            exchange(side, order)
            for element in range(elems):
                rows = rows_of(element)
                image = applied(side, element)
                before = r_ref[rows, :] if order == 0 else current[rows, :]
                keep(rows, order, before - image)
                if order < SSTEP - 1:
                    current[rows, :] = image
                    ext[1 - side, element] = image.astype(jnp.bfloat16)

        products = lax.dot_general(
            basis[:, :WIDTH], basis[...], (((0,), (0,)), ((), ())),
            preferred_element_type=jnp.float32,
        )
        cross = products[:, WIDTH:]
        gram = products[:, :WIDTH] + cross + cross.T
        for shard in range(count):
            partial[shard] = gram[shard * share : (shard + 1) * share, :]
        for step in range(1, count):
            sum_copy(partial.at[peer(step)], arrived.at[step], step, 0).start()
        rest = pl.ds(1, count - 1)
        whole = sum_copy(partial.at[rest], arrived.at[rest], 1, 0)
        whole.wait_recv()
        reduced = partial[me]
        for step in range(1, count):
            reduced = reduced + arrived[step]
        total[me] = reduced
        for step in range(1, count):
            sum_copy(total.at[me], total.at[me], step, 1).start()
        whole.wait_send()
        both = sum_copy(total.at[rest], total.at[rest], 1, 1)
        both.wait_recv()
        both.wait_send()
        system = jnp.concatenate(
            [total[shard] for shard in range(count)], axis=0
        )[:KEPT]
        coeffs = gauss_jordan(system)

        c0, c1, c2 = coeffs[:RHS], coeffs[RHS : 2 * RHS], coeffs[2 * RHS :]
        nothing = jnp.zeros((RHS, RHS), jnp.float32)
        late = c1 + c2
        down = jnp.concatenate([c0, c1, c2, nothing], axis=0)
        up = jnp.concatenate([-late, -c2, nothing, c0 + late], axis=0)
        high, low = split(jnp.concatenate([down, up], axis=1))
        factor = jnp.concatenate(
            [
                jnp.concatenate([high, low], axis=1),
                jnp.concatenate([high, jnp.zeros_like(low)], axis=1),
            ],
            axis=0,
        )
        for element in range(elems):
            rows = rows_of(element)
            change = jnp.dot(basis[rows, :], factor, preferred_element_type=jnp.float32)
            change = change[:, : 2 * RHS] + change[:, 2 * RHS :]
            x_ref[rows, :] = x_ref[rows, :] + change[:, RHS:]
            later = r_ref[rows, :] - change[:, :RHS]
            r_ref[rows, :] = later
            ext[0, element] = keep(rows, SSTEP, later)
        return carry

    lax.fori_loop(0, CYCLES, cycle, 0)


def shards(leaves, subs, right_side, first_guess, couple, send_lists, neighbours):
    elems, _, _ = couple.shape
    slots = send_lists.shape[2]
    count = leaves * subs
    share = WIDTH // count
    rows = elems * DOF
    vmem = pl.BlockSpec(memory_space=pltpu.VMEM)
    smem = pl.BlockSpec(memory_space=pltpu.SMEM)
    field = jax.ShapeDtypeStruct((rows, RHS), jnp.float32)
    x, r = pl.pallas_call(
        functools.partial(kernel, leaves, subs, elems, slots),
        out_shape=(field, field),
        in_specs=[vmem, vmem, vmem, smem, smem],
        out_specs=(vmem, vmem),
        scratch_shapes=[
            pltpu.VMEM((2, elems + 2 * slots + 1, DOF, RHS), jnp.bfloat16),
            pltpu.VMEM((rows, 2 * WIDTH), jnp.bfloat16),
            pltpu.VMEM((rows, RHS), jnp.float32),
            pltpu.VMEM((SSTEP + 1, 2, DOF, slots * RHS), jnp.bfloat16),
            pltpu.VMEM((SSTEP + 1, 2, DOF, slots * RHS), jnp.bfloat16),
            pltpu.VMEM((count, share, WIDTH), jnp.float32),
            pltpu.VMEM((count, share, WIDTH), jnp.float32),
            pltpu.VMEM((count, share, WIDTH), jnp.float32),
            pltpu.SemaphoreType.DMA((SSTEP + 1, 2)),
            pltpu.SemaphoreType.DMA((SSTEP + 1, 2)),
            pltpu.SemaphoreType.DMA((2,)),
            pltpu.SemaphoreType.DMA((2,)),
        ],
        compiler_params=pltpu.CompilerParams(
            collective_id=0, has_side_effects=True, vmem_limit_bytes=40 * 1024 * 1024
        ),
    )(
        right_side.reshape(rows, RHS), first_guess.reshape(rows, RHS),
        couple, send_lists, neighbours,
    )
    return x.reshape(right_side.shape), r.reshape(right_side.shape)


def solution(mesh):
    lead = ("grp", "leaf", "sub")
    flat, deep = P(lead, None), P(lead, None, None)
    return jax.shard_map(
        functools.partial(shards, mesh.shape["leaf"], mesh.shape["sub"]),
        mesh=mesh,
        in_specs=(flat, flat, deep, deep, flat),
        out_specs=(flat, flat),
        check_vma=False,
    )
```

```python
import functools

import jax
import jax.numpy as jnp
from jax import lax
from jax.experimental import pallas as pl
from jax.experimental.pallas import tpu as pltpu
from jax.sharding import PartitionSpec as P

DOF = 64
FACES = 6
RHS = 32
SSTEP = 3
CYCLES = 4
KEPT = SSTEP * RHS
WIDTH = KEPT + RHS
MESH = pl.DeviceIdType.MESH


def gauss_jordan(system):
    tile = 8
    tiles = [system[first : first + tile] for first in range(0, KEPT, tile)]
    rows = lax.broadcasted_iota(jnp.int32, (tile, WIDTH), 0)

    def columns(value, at):
        first = at * tile
        return [
            jnp.broadcast_to(value[:, first + k : first + k + 1], (tile, WIDTH))
            for k in range(tile)
        ]

    for at in range(len(tiles)):
        block, factors = tiles[at], columns(tiles[at], at)
        outside = [columns(value, at) if i != at else None for i, value in enumerate(tiles)]
        for k in range(tile):
            inverse = 1.0 / factors[k][k : k + 1, :]

            def eliminated(value):
                pivot_row = value[k : k + 1, :] * inverse
                return jnp.where(rows == k, pivot_row, value - factors[k] * pivot_row)

            block = eliminated(block)
            factors = factors[: k + 1] + [eliminated(value) for value in factors[k + 1 :]]
        tiles[at] = block
        for i in range(len(tiles)):
            if i != at:
                value = tiles[i]
                for k in range(tile):
                    value = value - outside[i][k] * block[k : k + 1, :]
                tiles[i] = value
    return jnp.concatenate(tiles, axis=0)[:, KEPT:]


def split(value):
    high = value.astype(jnp.bfloat16)
    return high, (value - high.astype(jnp.float32)).astype(jnp.bfloat16)


def kernel(
    leaves, subs, elems, slots,
    right_ref, guess_ref, couple_ref, lists_ref, near_ref,
    x_ref, r_ref,
    ext, basis, current, power_one, power_two, packed_out, packed_in, partial, arrived, total,
    halo_send, halo_recv, sum_send, sum_recv,
):
    count = leaves * subs
    share = WIDTH // count
    zero_at = elems + 2 * slots
    grp, leaf, sub = (lax.axis_index(name) for name in ("grp", "leaf", "sub"))
    me = leaf * subs + sub
    steps = [(far, near) for far in range(leaves) for near in range(subs)][1:]

    def turned(value, step, size):
        moved = value + step
        return jnp.where(moved >= size, moved - size, moved)

    def place(step):
        return (grp, turned(leaf, step[0], leaves), turned(sub, step[1], subs))

    def peer(step):
        return turned(leaf, step[0], leaves) * subs + turned(sub, step[1], subs)

    last_sub, first_sub = sub == subs - 1, sub == 0
    following = (
        grp, turned(leaf, jnp.where(last_sub, 1, 0), leaves), jnp.where(last_sub, 0, sub + 1)
    )
    preceding = (
        grp,
        turned(leaf, jnp.where(first_sub, leaves - 1, 0), leaves),
        jnp.where(first_sub, subs - 1, sub - 1),
    )

    barrier = pltpu.get_barrier_semaphore()
    for step in steps:
        pl.semaphore_signal(barrier, inc=1, device_id=place(step), device_id_type=MESH)
    pl.semaphore_wait(barrier, count - 1)

    for side in range(2):
        ext[side, elems:] = jnp.zeros((2 * slots + 1, DOF, RHS), jnp.bfloat16)

    def halo_copy(way, at, target):
        return pltpu.make_async_remote_copy(
            src_ref=packed_out.at[at, way],
            dst_ref=packed_in.at[at, way],
            send_sem=halo_send.at[at, way],
            recv_sem=halo_recv.at[at, way],
            device_id=target,
            device_id_type=MESH,
        )

    def exchange(side, at):
        for way in range(2):
            blocks = []
            for slot in range(slots):
                listed = lists_ref[0, way, slot]
                blocks.append(ext[side, jnp.where(listed < 0, zero_at, listed)])
            packed_out[at, way] = jnp.concatenate(blocks, axis=1)
        ahead = halo_copy(0, at, following)
        back = halo_copy(1, at, preceding)
        has_next = me < count - 1
        has_previous = me > 0

        @pl.when(has_next)
        def _():
            ahead.start()

        @pl.when(has_previous)
        def _():
            back.start()

        @pl.when(has_previous)
        def _():
            ahead.wait_recv()
            for slot in range(slots):
                ext[side, elems + slot] = packed_in[at, 0, :, slot * RHS : (slot + 1) * RHS]

        @pl.when(has_next)
        def _():
            back.wait_recv()
            for slot in range(slots):
                ext[side, elems + slots + slot] = packed_in[at, 1, :, slot * RHS : (slot + 1) * RHS]

        @pl.when(has_next)
        def _():
            ahead.wait_send()

        @pl.when(has_previous)
        def _():
            back.wait_send()

    def applied(side, element):
        blocks = []
        for face in range(FACES):
            near = near_ref[element, face]
            blocks.append(ext[side, jnp.where(near < 0, zero_at, near)])
        gathered = jnp.concatenate(blocks, axis=0)
        return jnp.dot(couple_ref[element], gathered, preferred_element_type=jnp.float32)

    def rows_of(element):
        return slice(element * DOF, (element + 1) * DOF)

    def keep(rows, order, value):
        high, low = split(value)
        if order <= SSTEP:
            at, below = order * RHS, WIDTH + order * RHS
        else:
            at = 2 * WIDTH + (order - SSTEP - 1) * RHS
            below = at + 2 * RHS
        basis[rows, at : at + RHS] = high
        basis[rows, below : below + RHS] = low
        return high

    def advance(side, at, order, store):
        exchange(side, at)
        for element in range(elems):
            rows = rows_of(element)
            image = applied(side, element)
            keep(rows, order, current[rows, :] - image)
            if store:
                current[rows, :] = image
                ext[1 - side, element] = image.astype(jnp.bfloat16)

    for element in range(elems):
        guess = guess_ref[rows_of(element), :]
        x_ref[rows_of(element), :] = guess
        ext[1, element] = guess.astype(jnp.bfloat16)
    exchange(1, SSTEP)
    for element in range(elems):
        rows = rows_of(element)
        first = right_ref[rows, :] - guess_ref[rows, :] + applied(1, element)
        r_ref[rows, :] = first
        ext[0, element] = keep(rows, SSTEP, first)

    exchange(0, 0)
    for element in range(elems):
        rows = rows_of(element)
        image = applied(0, element)
        keep(rows, 0, r_ref[rows, :] - image)
        power_one[rows, :] = image
        ext[1, element] = image.astype(jnp.bfloat16)
    exchange(1, 1)
    for element in range(elems):
        rows = rows_of(element)
        image = applied(1, element)
        keep(rows, 1, power_one[rows, :] - image)
        power_two[rows, :] = image
        current[rows, :] = image
        ext[0, element] = image.astype(jnp.bfloat16)

    def sum_copy(source, target, step, phase):
        return pltpu.make_async_remote_copy(
            src_ref=source,
            dst_ref=target,
            send_sem=sum_send.at[phase],
            recv_sem=sum_recv.at[phase],
            device_id=place(step),
            device_id_type=MESH,
        )

    def cycle(repeat, carry):
        advance(0, 0, 2, True)
        products = lax.dot_general(
            basis[:, :WIDTH], basis[:, : 2 * WIDTH], (((0,), (0,)), ((), ())),
            preferred_element_type=jnp.float32,
        )
        cross = products[:, WIDTH:]
        gram = products[:, :WIDTH] + cross + cross.T
        for shard in range(count):
            partial[shard] = gram[shard * share : (shard + 1) * share, :]
        for slot, step in enumerate(steps):
            sum_copy(partial.at[peer(step)], arrived.at[slot + 1], step, 0).start()
        rest = pl.ds(1, count - 1)
        whole = sum_copy(partial.at[rest], arrived.at[rest], steps[0], 0)
        advance(1, 1, 4, True)
        whole.wait_recv()
        reduced = partial[me]
        for step in range(1, count):
            reduced = reduced + arrived[step]
        total[me] = reduced
        for step in steps:
            sum_copy(total.at[me], total.at[me], step, 1).start()
        whole.wait_send()
        both = sum_copy(total.at[rest], total.at[rest], steps[0], 1)
        advance(0, 2, 5, False)
        both.wait_recv()
        both.wait_send()
        system = jnp.concatenate(
            [total[shard] for shard in range(count)], axis=0
        )[:KEPT]
        coeffs = gauss_jordan(system)

        c0, c1, c2 = coeffs[:RHS], coeffs[RHS : 2 * RHS], coeffs[2 * RHS :]
        nothing = jnp.zeros((RHS, RHS), jnp.float32)
        late = c1 + c2
        factor = jnp.concatenate(
            [
                jnp.concatenate([c0, c1, c2, nothing, nothing, nothing], axis=0),
                jnp.concatenate([-late, -c2, nothing, c0 + late, nothing, nothing], axis=0),
                jnp.concatenate([nothing, c0, c1, nothing, c2, nothing], axis=0),
                jnp.concatenate([nothing, nothing, c0, nothing, c1, c2], axis=0),
            ],
            axis=1,
        )
        high, low = split(factor)
        left = jnp.concatenate([high[:WIDTH], high[:WIDTH], high[WIDTH:], high[WIDTH:]], axis=0)
        right = jnp.concatenate(
            [low[:WIDTH], jnp.zeros_like(low[:WIDTH]), low[WIDTH:], jnp.zeros_like(low[WIDTH:])],
            axis=0,
        )
        factor = jnp.concatenate([left, right], axis=1)
        for element in range(elems):
            rows = rows_of(element)
            change = jnp.dot(basis[rows, :], factor, preferred_element_type=jnp.float32)
            change = change[:, :WIDTH] + change[:, WIDTH:]
            x_ref[rows, :] = x_ref[rows, :] + change[:, RHS : 2 * RHS]
            later = r_ref[rows, :] - change[:, :RHS]
            one = power_one[rows, :] - change[:, 2 * RHS : 3 * RHS]
            two = power_two[rows, :] - change[:, 3 * RHS :]
            r_ref[rows, :] = later
            power_one[rows, :] = one
            power_two[rows, :] = two
            current[rows, :] = two
            ext[0, element] = two.astype(jnp.bfloat16)
            keep(rows, SSTEP, later)
            keep(rows, 0, later - one)
            keep(rows, 1, one - two)
        return carry

    lax.fori_loop(0, CYCLES, cycle, 0)


def shards(leaves, subs, right_side, first_guess, couple, send_lists, neighbours):
    elems, _, _ = couple.shape
    slots = send_lists.shape[2]
    count = leaves * subs
    share = WIDTH // count
    rows = elems * DOF
    vmem = pl.BlockSpec(memory_space=pltpu.VMEM)
    smem = pl.BlockSpec(memory_space=pltpu.SMEM)
    field = jax.ShapeDtypeStruct((rows, RHS), jnp.float32)
    x, r = pl.pallas_call(
        functools.partial(kernel, leaves, subs, elems, slots),
        out_shape=(field, field),
        in_specs=[vmem, vmem, vmem, smem, smem],
        out_specs=(vmem, vmem),
        scratch_shapes=[
            pltpu.VMEM((2, elems + 2 * slots + 1, DOF, RHS), jnp.bfloat16),
            pltpu.VMEM((rows, 2 * WIDTH + 4 * RHS), jnp.bfloat16),
            pltpu.VMEM((rows, RHS), jnp.float32),
            pltpu.VMEM((rows, RHS), jnp.float32),
            pltpu.VMEM((rows, RHS), jnp.float32),
            pltpu.VMEM((SSTEP + 1, 2, DOF, slots * RHS), jnp.bfloat16),
            pltpu.VMEM((SSTEP + 1, 2, DOF, slots * RHS), jnp.bfloat16),
            pltpu.VMEM((count, share, WIDTH), jnp.float32),
            pltpu.VMEM((count, share, WIDTH), jnp.float32),
            pltpu.VMEM((count, share, WIDTH), jnp.float32),
            pltpu.SemaphoreType.DMA((SSTEP + 1, 2)),
            pltpu.SemaphoreType.DMA((SSTEP + 1, 2)),
            pltpu.SemaphoreType.DMA((2,)),
            pltpu.SemaphoreType.DMA((2,)),
        ],
        compiler_params=pltpu.CompilerParams(
            collective_id=0, has_side_effects=True, vmem_limit_bytes=40 * 1024 * 1024
        ),
    )(
        right_side.reshape(rows, RHS), first_guess.reshape(rows, RHS),
        couple, send_lists, neighbours,
    )
    return x.reshape(right_side.shape), r.reshape(right_side.shape)


def solution(mesh):
    lead = ("grp", "leaf", "sub")
    flat, deep = P(lead, None), P(lead, None, None)
    return jax.shard_map(
        functools.partial(shards, mesh.shape["leaf"], mesh.shape["sub"]),
        mesh=mesh,
        in_specs=(flat, flat, deep, deep, flat),
        out_specs=(flat, flat),
        check_vma=False,
    )
```

```python
import functools

import jax
import jax.numpy as jnp
from jax import lax
from jax.experimental import pallas as pl
from jax.experimental.pallas import tpu as pltpu
from jax.sharding import PartitionSpec as P

DOF = 64
FACES = 6
RHS = 32
SSTEP = 3
CYCLES = 4
KEPT = SSTEP * RHS
WIDTH = KEPT + RHS
MESH = pl.DeviceIdType.MESH


def gauss_jordan(system):
    tile = 8
    tiles = [system[first : first + tile] for first in range(0, KEPT, tile)]
    rows = lax.broadcasted_iota(jnp.int32, (tile, WIDTH), 0)

    def columns(value, at):
        first = at * tile
        return [
            jnp.broadcast_to(value[:, first + k : first + k + 1], (tile, WIDTH))
            for k in range(tile)
        ]

    for at in range(len(tiles)):
        block, factors = tiles[at], columns(tiles[at], at)
        outside = [columns(value, at) if i != at else None for i, value in enumerate(tiles)]
        for k in range(tile):
            inverse = 1.0 / factors[k][k : k + 1, :]

            def eliminated(value):
                pivot_row = value[k : k + 1, :] * inverse
                return jnp.where(rows == k, pivot_row, value - factors[k] * pivot_row)

            block = eliminated(block)
            factors = factors[: k + 1] + [eliminated(value) for value in factors[k + 1 :]]
        tiles[at] = block
        for i in range(len(tiles)):
            if i != at:
                value = tiles[i]
                for k in range(tile):
                    value = value - outside[i][k] * block[k : k + 1, :]
                tiles[i] = value
    return jnp.concatenate(tiles, axis=0)[:, KEPT:]


def split(value):
    high = value.astype(jnp.bfloat16)
    return high, (value - high.astype(jnp.float32)).astype(jnp.bfloat16)


def kernel(
    leaves, subs, elems, slots,
    right_ref, guess_ref, couple_ref, lists_ref, near_ref,
    x_ref, r_ref,
    ext, basis, current, power_one, power_two, packed_out, packed_in, partial, arrived, total,
    halo_send, halo_recv, sum_send, sum_recv,
):
    count = leaves * subs
    share = WIDTH // count
    zero_at = elems + 2 * slots
    grp, leaf, sub = (lax.axis_index(name) for name in ("grp", "leaf", "sub"))
    me = leaf * subs + sub
    steps = [(far, near) for far in range(leaves) for near in range(subs)][1:]

    def turned(value, step, size):
        moved = value + step
        return jnp.where(moved >= size, moved - size, moved)

    def place(step):
        return (grp, turned(leaf, step[0], leaves), turned(sub, step[1], subs))

    def peer(step):
        return turned(leaf, step[0], leaves) * subs + turned(sub, step[1], subs)

    last_sub, first_sub = sub == subs - 1, sub == 0
    following = (
        grp, turned(leaf, jnp.where(last_sub, 1, 0), leaves), jnp.where(last_sub, 0, sub + 1)
    )
    preceding = (
        grp,
        turned(leaf, jnp.where(first_sub, leaves - 1, 0), leaves),
        jnp.where(first_sub, subs - 1, sub - 1),
    )

    barrier = pltpu.get_barrier_semaphore()
    for step in steps:
        pl.semaphore_signal(barrier, inc=1, device_id=place(step), device_id_type=MESH)
    pl.semaphore_wait(barrier, count - 1)

    for side in range(2):
        ext[side, elems:] = jnp.zeros((2 * slots + 1, DOF, RHS), jnp.bfloat16)

    def halo_copy(way, at, target):
        return pltpu.make_async_remote_copy(
            src_ref=packed_out.at[at, way],
            dst_ref=packed_in.at[at, way],
            send_sem=halo_send.at[at, way],
            recv_sem=halo_recv.at[at, way],
            device_id=target,
            device_id_type=MESH,
        )

    def exchange(side, at, meanwhile=None):
        def pack(way):
            blocks = []
            for slot in range(slots):
                listed = lists_ref[0, way, slot]
                blocks.append(ext[side, jnp.where(listed < 0, zero_at, listed)])
            packed_out[at, way] = jnp.concatenate(blocks, axis=1)

        ahead = halo_copy(0, at, following)
        back = halo_copy(1, at, preceding)
        has_next = me < count - 1
        has_previous = me > 0
        pack(0)

        @pl.when(has_next)
        def _():
            ahead.start()

        pack(1)

        @pl.when(has_previous)
        def _():
            back.start()

        if meanwhile is not None:
            meanwhile()

        @pl.when(has_previous)
        def _():
            ahead.wait_recv()
            for slot in range(slots):
                ext[side, elems + slot] = packed_in[at, 0, :, slot * RHS : (slot + 1) * RHS]

        @pl.when(has_next)
        def _():
            back.wait_recv()
            for slot in range(slots):
                ext[side, elems + slots + slot] = packed_in[at, 1, :, slot * RHS : (slot + 1) * RHS]

        @pl.when(has_next)
        def _():
            ahead.wait_send()

        @pl.when(has_previous)
        def _():
            back.wait_send()

    def applied(side, element):
        blocks = []
        for face in range(FACES):
            near = near_ref[element, face]
            blocks.append(ext[side, jnp.where(near < 0, zero_at, near)])
        gathered = jnp.concatenate(blocks, axis=0)
        return jnp.dot(couple_ref[element], gathered, preferred_element_type=jnp.float32)

    def rows_of(element):
        return slice(element * DOF, (element + 1) * DOF)

    def keep(rows, order, value):
        high, low = split(value)
        if order <= SSTEP:
            at, below = order * RHS, WIDTH + order * RHS
        else:
            at = 2 * WIDTH + (order - SSTEP - 1) * RHS
            below = at + 2 * RHS
        basis[rows, at : at + RHS] = high
        basis[rows, below : below + RHS] = low
        return high

    def advance(side, at, order, store, meanwhile=None):
        exchange(side, at, meanwhile)
        for element in range(elems):
            rows = rows_of(element)
            image = applied(side, element)
            keep(rows, order, current[rows, :] - image)
            if store:
                current[rows, :] = image
                ext[1 - side, element] = image.astype(jnp.bfloat16)

    for element in range(elems):
        guess = guess_ref[rows_of(element), :]
        x_ref[rows_of(element), :] = guess
        ext[1, element] = guess.astype(jnp.bfloat16)
    exchange(1, SSTEP)
    for element in range(elems):
        rows = rows_of(element)
        first = right_ref[rows, :] - guess_ref[rows, :] + applied(1, element)
        r_ref[rows, :] = first
        ext[0, element] = first.astype(jnp.bfloat16)

    exchange(0, 0)
    for element in range(elems):
        rows = rows_of(element)
        image = applied(0, element)
        power_one[rows, :] = image
        ext[1, element] = image.astype(jnp.bfloat16)
    exchange(1, 1)
    for element in range(elems):
        rows = rows_of(element)
        image = applied(1, element)
        power_two[rows, :] = image
        current[rows, :] = image
        ext[0, element] = image.astype(jnp.bfloat16)

    def sum_copy(source, target, step, phase):
        return pltpu.make_async_remote_copy(
            src_ref=source,
            dst_ref=target,
            send_sem=sum_send.at[phase],
            recv_sem=sum_recv.at[phase],
            device_id=place(step),
            device_id_type=MESH,
        )

    def refresh():
        for element in range(elems):
            rows = rows_of(element)
            zero, one, two = r_ref[rows, :], power_one[rows, :], power_two[rows, :]
            keep(rows, SSTEP, zero)
            keep(rows, 0, zero - one)
            keep(rows, 1, one - two)

    def cycle(repeat, carry):
        advance(0, 0, 2, True, refresh)
        products = lax.dot_general(
            basis[:, :WIDTH], basis[:, : 2 * WIDTH], (((0,), (0,)), ((), ())),
            preferred_element_type=jnp.float32,
        )
        cross = products[:, WIDTH:]
        gram = products[:, :WIDTH] + cross + cross.T
        for shard in range(count):
            partial[shard] = gram[shard * share : (shard + 1) * share, :]
        for slot, step in enumerate(steps):
            sum_copy(partial.at[peer(step)], arrived.at[slot + 1], step, 0).start()
        rest = pl.ds(1, count - 1)
        whole = sum_copy(partial.at[rest], arrived.at[rest], steps[0], 0)
        advance(1, 1, 4, True)
        whole.wait_recv()
        reduced = partial[me]
        for step in range(1, count):
            reduced = reduced + arrived[step]
        total[me] = reduced
        for step in steps:
            sum_copy(total.at[me], total.at[me], step, 1).start()
        whole.wait_send()
        both = sum_copy(total.at[rest], total.at[rest], steps[0], 1)
        advance(0, 2, 5, False)
        both.wait_recv()
        both.wait_send()
        system = jnp.concatenate(
            [total[shard] for shard in range(count)], axis=0
        )[:KEPT]
        coeffs = gauss_jordan(system)

        c0, c1, c2 = coeffs[:RHS], coeffs[RHS : 2 * RHS], coeffs[2 * RHS :]
        nothing = jnp.zeros((RHS, RHS), jnp.float32)
        late = c1 + c2
        factor = jnp.concatenate(
            [
                jnp.concatenate([c0, c1, c2, nothing, nothing, nothing], axis=0),
                jnp.concatenate([-late, -c2, nothing, c0 + late, nothing, nothing], axis=0),
                jnp.concatenate([nothing, c0, c1, nothing, c2, nothing], axis=0),
                jnp.concatenate([nothing, nothing, c0, nothing, c1, c2], axis=0),
            ],
            axis=1,
        )
        high, low = split(factor)
        left = jnp.concatenate([high[:WIDTH], high[:WIDTH], high[WIDTH:], high[WIDTH:]], axis=0)
        right = jnp.concatenate(
            [low[:WIDTH], jnp.zeros_like(low[:WIDTH]), low[WIDTH:], jnp.zeros_like(low[WIDTH:])],
            axis=0,
        )
        factor = jnp.concatenate([left, right], axis=1)
        for element in range(elems):
            rows = rows_of(element)
            change = jnp.dot(basis[rows, :], factor, preferred_element_type=jnp.float32)
            change = change[:, :WIDTH] + change[:, WIDTH:]
            x_ref[rows, :] = x_ref[rows, :] + change[:, RHS : 2 * RHS]
            later = r_ref[rows, :] - change[:, :RHS]
            one = power_one[rows, :] - change[:, 2 * RHS : 3 * RHS]
            two = power_two[rows, :] - change[:, 3 * RHS :]
            r_ref[rows, :] = later
            power_one[rows, :] = one
            power_two[rows, :] = two
            current[rows, :] = two
            ext[0, element] = two.astype(jnp.bfloat16)
        return carry

    lax.fori_loop(0, CYCLES, cycle, 0)


def shards(leaves, subs, right_side, first_guess, couple, send_lists, neighbours):
    elems, _, _ = couple.shape
    slots = send_lists.shape[2]
    count = leaves * subs
    share = WIDTH // count
    rows = elems * DOF
    vmem = pl.BlockSpec(memory_space=pltpu.VMEM)
    smem = pl.BlockSpec(memory_space=pltpu.SMEM)
    field = jax.ShapeDtypeStruct((rows, RHS), jnp.float32)
    x, r = pl.pallas_call(
        functools.partial(kernel, leaves, subs, elems, slots),
        out_shape=(field, field),
        in_specs=[vmem, vmem, vmem, smem, smem],
        out_specs=(vmem, vmem),
        scratch_shapes=[
            pltpu.VMEM((2, elems + 2 * slots + 1, DOF, RHS), jnp.bfloat16),
            pltpu.VMEM((rows, 2 * WIDTH + 4 * RHS), jnp.bfloat16),
            pltpu.VMEM((rows, RHS), jnp.float32),
            pltpu.VMEM((rows, RHS), jnp.float32),
            pltpu.VMEM((rows, RHS), jnp.float32),
            pltpu.VMEM((SSTEP + 1, 2, DOF, slots * RHS), jnp.bfloat16),
            pltpu.VMEM((SSTEP + 1, 2, DOF, slots * RHS), jnp.bfloat16),
            pltpu.VMEM((count, share, WIDTH), jnp.float32),
            pltpu.VMEM((count, share, WIDTH), jnp.float32),
            pltpu.VMEM((count, share, WIDTH), jnp.float32),
            pltpu.SemaphoreType.DMA((SSTEP + 1, 2)),
            pltpu.SemaphoreType.DMA((SSTEP + 1, 2)),
            pltpu.SemaphoreType.DMA((2,)),
            pltpu.SemaphoreType.DMA((2,)),
        ],
        compiler_params=pltpu.CompilerParams(
            collective_id=0, has_side_effects=True, vmem_limit_bytes=40 * 1024 * 1024
        ),
    )(
        right_side.reshape(rows, RHS), first_guess.reshape(rows, RHS),
        couple, send_lists, neighbours,
    )
    return x.reshape(right_side.shape), r.reshape(right_side.shape)


def solution(mesh):
    lead = ("grp", "leaf", "sub")
    flat, deep = P(lead, None), P(lead, None, None)
    return jax.shard_map(
        functools.partial(shards, mesh.shape["leaf"], mesh.shape["sub"]),
        mesh=mesh,
        in_specs=(flat, flat, deep, deep, flat),
        out_specs=(flat, flat),
        check_vma=False,
    )
```
